32 devices in a mesh: req: 8 (over z, x), head: 4 (over y, core).
Axes of the slice: x: 2, y: 2, z: 4, core: 2. Of those that a mesh axis runs over, the one named last changes fastest.
Arguments:
- tokens: bfloat16 [384, 1024], P('req'), may hold values from -6 to 6
- cache_len: int32 [384], P('req'), may hold values from 1 to 1024, as said below
- page_table: int32 [384, 8], P('req'), may hold values from 0 to 159, as said below
- page_live: int32 [384, 8], P('req'), may hold values 0 or 1
- group_of: int32 [384], replicated, may hold values from 0 to 31, as said below
- kv_pool: bfloat16 [1280, 128, 2, 1024], P('req', None, None, 'head')
- enc_kv: bfloat16 [32, 2048, 2, 1024], P('req', None, None, 'head')
- w_self_in: bfloat16 [1024, 3, 1024], P('req', None, 'head'), may hold values from -0.1875 to 0.1875
- w_self_out: bfloat16 [1024, 1024], P('head', 'req'), may hold values from -0.75 to 0.75
- w_cross_q: bfloat16 [1024, 1024], P('req', 'head'), may hold values from -0.1875 to 0.1875
- w_cross_out: bfloat16 [1024, 1024], P('head', 'req'), may hold values from -0.75 to 0.75
- self_gain: float32 [1024], replicated, may hold values from 0.25 to 1.75
- self_bias: float32 [1024], replicated, may hold values from -1.75 to 1.75
- cross_gain: float32 [1024], replicated, may hold values from 0.25 to 1.75
- cross_bias: float32 [1024], replicated, may hold values from -1.75 to 1.75
Outputs:
- hidden_out: bfloat16 [384, 1024], P('req')
- new_kv: bfloat16 [384, 2, 1024], P('req', None, 'head')
The draws below stay inside these ranges and needn't reach their ends.
Inputs may be any that keep to these rules, and one draw needn't show every extreme that they name: The pages of one device's requests, ceil(cache_len / 128) each, add up to at most 160; some request holds 1024 positions. `page_table`: for request r the slots j < ceil(cache_len[r] / 128) name pages of the pool part of r's index of req; no page is named by two such slots. Other slots hold any page number. `group_of`: every group has 8 to 16 requests; some group has exactly 16 and some exactly 8.
All inputs are finite; a program needn't handle non-finite values. No bound on the sum of `page_live` on one device may be relied on, other than what follows from the above.
Results may differ from the reference program's by a relative error of at most 0.019.
The reference program's roundings to bfloat16 on the way count: a program that leaves them out, or rounds other values in their place, can miss the bound.
Values may be sent and summed in bfloat16 or wider, within the bound.
A program may use at most 128 MiB of HBM per device.

```python
import jax
import jax.numpy as jnp
from jax import lax

D = 1024
HEADS = 16
HEAD_DIM = 64
R_DEV = 48
PAGE = 128
MAXP = 8
PAGES_DEV = 160
ENC = 2048
GMAX = 16
REQ = 384
GROUPS = 32


def lengths_drawn(key):
    devices = REQ // R_DEV
    spare_pages = min((PAGES_DEV - MAXP) // (R_DEV - 1), MAXP)
    splits = jax.random.split(jax.random.fold_in(key, 11), 5)
    counts = jax.random.randint(splits[0], (REQ,), 1, spare_pages + 1)
    flags = jax.random.randint(splits[1], (devices,), 0, 2)
    forced = jax.random.randint(splits[2], (), 0, devices)
    flags = jnp.where(jnp.arange(devices) == forced, 1, flags)
    chosen_slot = jax.random.randint(splits[3], (devices,), 0, R_DEV)
    request_ids = jnp.arange(REQ)
    device_ids = request_ids // R_DEV
    longest = (request_ids % R_DEV == chosen_slot[device_ids]) & (flags[device_ids] == 1)
    counts = jnp.where(longest, MAXP, counts)
    tail_rows = jnp.where(longest, PAGE, jax.random.randint(splits[4], (REQ,), 1, PAGE + 1))
    return ((counts - 1) * PAGE + tail_rows).astype(jnp.int32)


def draw_cache_len(key, part):
    return lengths_drawn(key)


def draw_page_table(key, part):
    lengths = lengths_drawn(key)
    counts = (lengths + PAGE - 1) // PAGE
    devices = REQ // R_DEV
    perm_keys = jax.random.split(jax.random.fold_in(key, 12), devices)
    orders = jax.vmap(lambda one: jax.random.permutation(one, PAGES_DEV))(perm_keys)
    per_device = counts.reshape(devices, R_DEV)
    offsets = (jnp.cumsum(per_device, axis=1) - per_device).reshape(REQ)
    columns = jnp.arange(MAXP)
    position = jnp.minimum(offsets[:, None] + columns[None, :], PAGES_DEV - 1)
    owner_rows = orders[jnp.arange(REQ) // R_DEV]
    chosen = jnp.take_along_axis(owner_rows, position, axis=1)
    filler = jax.random.randint(jax.random.fold_in(key, 13), (REQ, MAXP), 0, PAGES_DEV)
    return jnp.where(columns[None, :] < counts[:, None], chosen, filler).astype(jnp.int32)


def draw_group_of(key, part):
    mean_size = REQ // GROUPS
    reach = GMAX - mean_size
    splits = jax.random.split(jax.random.fold_in(key, 14), 3)
    shifts = jax.random.randint(splits[0], (GROUPS // 2,), -reach, reach + 1)
    forced = jax.random.randint(splits[1], (), 0, GROUPS // 2)
    shifts = jnp.where(jnp.arange(GROUPS // 2) == forced, reach, shifts)
    group_sizes = jnp.stack([mean_size + shifts, mean_size - shifts], axis=1).reshape(GROUPS)
    labels = jnp.repeat(jnp.arange(GROUPS), group_sizes, total_repeat_length=REQ)
    return labels[jax.random.permutation(splits[2], REQ)].astype(jnp.int32)


def states_drawn(key, shape):
    base = jax.random.normal(jax.random.fold_in(key, 21), shape, jnp.float32)
    return base.astype(jnp.bfloat16)


def draw_kv_pool(key, part):
    return states_drawn(key, (REQ // R_DEV * PAGES_DEV, PAGE, 2, D))


def draw_enc_kv(key, part):
    return states_drawn(key, (GROUPS, ENC, 2, D))


def place_ends(drawn, own_key, low, top_value):
    dims = drawn.shape
    spot = [jax.random.randint(jax.random.fold_in(own_key, axis), (), 0, dims[axis]) for axis in range(len(dims))]
    drawn = drawn.at[tuple(spot)].set(low)
    longest = dims.index(max(dims))
    spot[longest] = (spot[longest] + 1) % dims[longest]
    return drawn.at[tuple(spot)].set(top_value)


def block_levels(own_key, dims, cuts, smallest, largest):
    level = 1.0
    for axis_at, parts in cuts:
        heights = jax.random.uniform(jax.random.fold_in(jax.random.fold_in(own_key, 6), axis_at), (parts,), jnp.float32, smallest / len(cuts), largest / len(cuts))
        level = level * jnp.repeat(jnp.exp(heights), dims[axis_at] // parts).reshape((-1,) + (1,) * (len(dims) - 1 - axis_at))
    return level


def scatter_about(stream_key, shape, width, limit, cuts=(), kind=jnp.bfloat16):
    entries = jax.random.normal(stream_key, shape, jnp.float32) * width
    if len(cuts) > 0:
        entries = block_levels(stream_key, shape, cuts, -0.22, 0.18) * entries
    return jnp.clip(entries, min=-limit, max=limit).astype(kind)


def setup_inputs(seed: int = 0) -> dict:
    key_of = jax.random.split(jax.random.key(seed), 16)
    tokens = scatter_about(key_of[0], (REQ, D), 1.0, 6.0, ((0, 8),))
    cache_len = draw_cache_len(jax.random.fold_in(key_of[15], 71), 0)
    page_table = draw_page_table(jax.random.fold_in(key_of[15], 71), 0)
    page_live = place_ends((jax.random.randint(key_of[3], (REQ, MAXP), 0, 8) < 7).astype(jnp.int32), jax.random.fold_in(key_of[3], 1), 0, 1)
    group_of = draw_group_of(jax.random.fold_in(key_of[15], 71), 0)
    kv_pool = draw_kv_pool(jax.random.fold_in(key_of[15], 71), 0)
    enc_kv = draw_enc_kv(jax.random.fold_in(key_of[15], 71), 0)
    w_self_in = scatter_about(key_of[7], (D, 3, D), D ** -0.5, 0.1875, ((0, 8), (2, 4)))
    w_self_out = scatter_about(key_of[8], (D, D), HEAD_DIM ** -0.5, 0.75, ((0, 4), (1, 8)))
    w_cross_q = scatter_about(key_of[9], (D, D), D ** -0.5, 0.1875, ((0, 8), (1, 4)))
    w_cross_out = scatter_about(key_of[10], (D, D), HEAD_DIM ** -0.5, 0.75, ((0, 4), (1, 8)))
    self_gain = jnp.clip(1.0 + 0.15 * jax.random.normal(key_of[11], (D,), jnp.float32), 0.25, 1.75)
    self_bias = scatter_about(key_of[12], (D,), 0.3, 1.75, (), jnp.float32)
    cross_gain = jnp.clip(1.0 + 0.15 * jax.random.normal(key_of[13], (D,), jnp.float32), 0.25, 1.75)
    cross_bias = scatter_about(key_of[14], (D,), 0.3, 1.75, (), jnp.float32)
    return dict(tokens=tokens, cache_len=cache_len, page_table=page_table, page_live=page_live, group_of=group_of, kv_pool=kv_pool, enc_kv=enc_kv, w_self_in=w_self_in, w_self_out=w_self_out, w_cross_q=w_cross_q, w_cross_out=w_cross_out, self_gain=self_gain, self_bias=self_bias, cross_gain=cross_gain, cross_bias=cross_bias)


def layer_norm(summed, gain_row, bias_row):
    center = summed - lax.optimization_barrier(jnp.mean(summed, axis=-1, keepdims=True))
    spread = lax.optimization_barrier(jnp.mean(center * center, axis=-1, keepdims=True))
    return center * lax.rsqrt(spread + 1e-05) * gain_row + bias_row

def reference(tokens, cache_len, page_table, page_live, group_of, kv_pool, enc_kv, w_self_in, w_self_out, w_cross_q, w_cross_out, self_gain, self_bias, cross_gain, cross_bias):
    scale = HEAD_DIM ** (-0.5)
    qkv = jnp.dot(tokens, w_self_in.reshape(D, 3 * D), preferred_element_type=jnp.float32)
    qkv = qkv.astype(jnp.bfloat16).reshape(REQ, 3, D)
    owner_dev = (jnp.arange(REQ, dtype=jnp.int32) // R_DEV).astype(jnp.int32)

    def self_one(items):
        query, new_key, new_value, length, table_row, live_row, owner = items
        pages = kv_pool[owner * PAGES_DEV + table_row]
        keys = pages[:, :, 0].reshape(MAXP * PAGE, HEADS, HEAD_DIM).astype(jnp.float32)
        values = pages[:, :, 1].reshape(MAXP * PAGE, HEADS, HEAD_DIM).astype(jnp.float32)
        position = jnp.arange(MAXP * PAGE, dtype=jnp.int32)
        counted = (position < length) & (jnp.repeat(live_row, PAGE) == 1)
        q_heads = query.astype(jnp.float32).reshape(HEADS, HEAD_DIM)
        scores = jnp.einsum('thd,hd->ht', keys, q_heads) * scale
        scores = jnp.where(counted[None, :], scores, -1e+30)
        new_score = lax.optimization_barrier(jnp.sum(q_heads * new_key.astype(jnp.float32).reshape(HEADS, HEAD_DIM), axis=-1)) * scale
        top = jnp.maximum(lax.optimization_barrier(jnp.max(scores, axis=1)), new_score)
        weights = jnp.where(counted[None, :], jnp.exp(scores - top[:, None]), 0.0)
        new_weight = jnp.exp(new_score - top)
        total = lax.optimization_barrier(jnp.sum(weights, axis=1)) + new_weight
        rounded = lax.optimization_barrier(weights.astype(jnp.bfloat16)).astype(jnp.float32)
        rounded_new = lax.optimization_barrier(new_weight.astype(jnp.bfloat16)).astype(jnp.float32)
        summed = jnp.einsum('ht,thd->hd', rounded, values)
        summed = summed + rounded_new[:, None] * new_value.astype(jnp.float32).reshape(HEADS, HEAD_DIM)
        return (summed / total[:, None]).reshape(D).astype(jnp.bfloat16)
    self_ctx = lax.map(self_one, (qkv[:, 0], qkv[:, 1], qkv[:, 2], cache_len, page_table, page_live, owner_dev))
    self_proj = jnp.dot(self_ctx, w_self_out, preferred_element_type=jnp.float32)
    h_first = layer_norm(tokens.astype(jnp.float32) + self_proj, self_gain, self_bias).astype(jnp.bfloat16)
    cross_q = jnp.dot(h_first, w_cross_q, preferred_element_type=jnp.float32).astype(jnp.bfloat16)

    def cross_one(items):
        query, group = items
        states = enc_kv[group]
        keys = states[:, 0].reshape(ENC, HEADS, HEAD_DIM).astype(jnp.float32)
        values = states[:, 1].reshape(ENC, HEADS, HEAD_DIM).astype(jnp.float32)
        q_heads = query.astype(jnp.float32).reshape(HEADS, HEAD_DIM)
        scores = jnp.einsum('ehd,hd->he', keys, q_heads) * scale
        top = lax.optimization_barrier(jnp.max(scores, axis=1))
        weights = jnp.exp(scores - top[:, None])
        total = lax.optimization_barrier(jnp.sum(weights, axis=1))
        rounded = lax.optimization_barrier(weights.astype(jnp.bfloat16)).astype(jnp.float32)
        summed = jnp.einsum('he,ehd->hd', rounded, values)
        return (summed / total[:, None]).reshape(D).astype(jnp.bfloat16)
    cross_ctx = lax.map(cross_one, (cross_q, group_of))
    cross_proj = jnp.dot(cross_ctx, w_cross_out, preferred_element_type=jnp.float32)
    hidden_out = layer_norm(h_first.astype(jnp.float32) + cross_proj, cross_gain, cross_bias).astype(jnp.bfloat16)
    return (hidden_out, qkv[:, 1:3])
```

```python
import functools

import jax
import jax.numpy as jnp
from jax import lax
from jax.experimental import pallas as pl
from jax.experimental.pallas import tpu as pltpu
from jax.sharding import PartitionSpec as P

HEAD_DIM = 64
GMAX = 16


def layer_norm(summed, gain_row, bias_row):
    center = summed - jnp.mean(summed, axis=-1, keepdims=True)
    spread = jnp.mean(center * center, axis=-1, keepdims=True)
    return center * lax.rsqrt(spread + 1e-05) * gain_row + bias_row


def head_total(partial_value):
    return lax.psum(partial_value, "head")


LANES = 128
NEG = -1e30
VMEM_LIMIT = 60 * 1024 * 1024


def pair_copies(source, rows, start, held, sems, slot):
    return [
        pltpu.make_async_copy(
            source.at[pl.ds(start, rows), pl.ds(half * LANES, LANES)],
            held.at[slot, half],
            sems.at[slot, half],
        )
        for half in range(held.shape[1])
    ]


def page_kernel(valid_ref, query_ref, kv_ref, acc_ref, top_ref, total_ref, held, sems, *, batch):
    pages, page_rows, _, cols = kv_ref.shape
    heads = cols // HEAD_DIM
    span = 2 * page_rows
    source = kv_ref.reshape(pages * span, cols)
    steps = pages // batch
    rows = batch * span
    slots = held.shape[0]
    for step in range(min(slots, steps)):
        for copy in pair_copies(source, rows, step * rows, held, sems, step):
            copy.start()
    head_row = lax.broadcasted_iota(jnp.int32, (8, cols), 0)
    head_mask = head_row == lax.broadcasted_iota(jnp.int32, (8, cols), 1) // HEAD_DIM
    column = lax.broadcasted_iota(jnp.int32, (8, span), 1)
    is_key = column % 2 == 0

    def body(step, carry):
        slot = lax.rem(step, slots)
        for copy in pair_copies(source, rows, step * rows, held, sems, slot):
            copy.wait()
        accs, tops, totals = [], [], []
        for page in range(batch):
            valid = valid_ref[step * batch + page]
            states = jnp.concatenate(
                [held[slot, half, pl.ds(page * span, span), :] for half in range(held.shape[1])], axis=1
            )
            query = query_ref[pl.ds(step * batch + page, 1), :]
            spread = jnp.where(head_mask, jnp.broadcast_to(query, (8, cols)), 0.0).astype(jnp.bfloat16)
            scores = lax.dot_general(
                spread, states, (((1,), (1,)), ((), ())), preferred_element_type=jnp.float32
            )
            counted = is_key & (column < 2 * valid)
            scores = jnp.where(counted, scores, NEG)
            top = jnp.max(scores, axis=1, keepdims=True)
            weights = jnp.where(counted, jnp.exp(scores - top), 0.0)
            total = jnp.sum(weights, axis=1, keepdims=True)
            moved = pltpu.roll(weights, 1, 1).astype(jnp.bfloat16)
            summed = jnp.dot(moved, states, preferred_element_type=jnp.float32)
            accs.append(jnp.sum(jnp.where(head_mask, summed, 0.0), axis=0, keepdims=True))
            tops.append(jnp.sum(jnp.where(head_mask, top, 0.0), axis=0, keepdims=True))
            totals.append(jnp.sum(jnp.where(head_mask, total, 0.0), axis=0, keepdims=True))
        here = pl.ds(pl.multiple_of(step * batch, batch), batch)
        acc_ref[here, :] = jnp.concatenate(accs, axis=0)
        top_ref[here, :] = jnp.concatenate(tops, axis=0)
        total_ref[here, :] = jnp.concatenate(totals, axis=0)

        @pl.when(step + slots < steps)
        def _():
            for copy in pair_copies(source, rows, (step + slots) * rows, held, sems, slot):
                copy.start()

        return carry

    lax.fori_loop(0, steps, body, 0)


def page_parts(page_valid, page_query, kv_pool):
    pages, page_rows, _, cols = kv_pool.shape
    batch = 8
    slots = min(8, pages // batch)
    part = jax.ShapeDtypeStruct((pages, cols), jnp.float32)
    return pl.pallas_call(
        functools.partial(page_kernel, batch=batch),
        out_shape=(part, part, part),
        in_specs=[
            pl.BlockSpec(memory_space=pltpu.SMEM),
            pl.BlockSpec(memory_space=pltpu.VMEM),
            pl.BlockSpec(memory_space=pl.ANY),
        ],
        out_specs=(pl.BlockSpec(memory_space=pltpu.VMEM),) * 3,
        scratch_shapes=[
            pltpu.VMEM((slots, cols // LANES, batch * 2 * page_rows, LANES), jnp.bfloat16),
            pltpu.SemaphoreType.DMA((slots, cols // LANES)),
        ],
        compiler_params=pltpu.CompilerParams(vmem_limit_bytes=VMEM_LIMIT),
        cost_estimate=pl.CostEstimate(
            flops=pages * 8 * 2 * page_rows * cols * 4,
            bytes_accessed=pages * page_rows * 4 * cols,
            transcendentals=pages * 16 * page_rows,
        ),
        name="page_parts",
    )(page_valid, page_query, kv_pool)


def paged_attention(query, new_key, new_value, cache_len, page_table, page_live, kv_pool, scale):
    pages_here, page_rows, _, head_cols = kv_pool.shape
    heads_here = head_cols // HEAD_DIM
    rows_here = query.shape[0]
    slots = page_table.shape[1]
    counts = (cache_len + page_rows - 1) // page_rows
    slot_index = jnp.arange(slots, dtype=jnp.int32)
    in_use = slot_index[None, :] < counts[:, None]
    hits = (
        page_table[:, :, None] == jnp.arange(pages_here, dtype=jnp.int32)[None, None, :]
    ) & in_use[:, :, None]
    owners = jnp.any(hits, axis=1)
    slot_valid = jnp.where(
        page_live == 1,
        jnp.clip(cache_len[:, None] - slot_index[None, :] * page_rows, 0, page_rows),
        0,
    )
    page_valid = jnp.sum(jnp.where(hits, slot_valid[:, :, None], 0), axis=(0, 1))
    owner_weights = owners.astype(jnp.float32)
    scaled = (query * scale).astype(jnp.bfloat16)
    page_query = jnp.dot(owners.T.astype(jnp.bfloat16), scaled, preferred_element_type=jnp.float32)
    page_sum, page_top, page_total = page_parts(page_valid, page_query, kv_pool)
    products = query.astype(jnp.float32) * new_key.astype(jnp.float32)
    new_score = jnp.sum(products.reshape(rows_here, heads_here, HEAD_DIM), axis=-1) * scale
    new_score = jnp.repeat(new_score, HEAD_DIM, axis=1)
    counted = owners & (page_valid > 0)[None, :]
    owner_top = jnp.max(jnp.where(counted[:, :, None], page_top[None, :, :], NEG), axis=1)
    top = jnp.maximum(owner_top, new_score)
    page_shift = jnp.dot(owner_weights.T, top, precision=lax.Precision.HIGHEST)
    factor = jnp.where((page_valid > 0)[:, None], jnp.exp(page_top - page_shift), 0.0)
    new_weight = jnp.exp(new_score - top)
    both = jnp.dot(
        owner_weights,
        jnp.concatenate([page_sum * factor, page_total * factor], axis=1),
        precision=lax.Precision.HIGHEST,
    )
    rounded_new = lax.optimization_barrier(new_weight.astype(jnp.bfloat16)).astype(jnp.float32)
    summed = both[:, :head_cols] + rounded_new * new_value.astype(jnp.float32)
    return (summed / (both[:, head_cols:] + new_weight)).astype(jnp.bfloat16)


def group_kernel(picker_ref, query_ref, kv_ref, out_ref, held, scores_ref, sems):
    groups, positions, _, cols = kv_ref.shape
    heads = cols // HEAD_DIM
    span = 2 * positions
    source = kv_ref.reshape(groups * span, cols)
    for group in range(groups):
        for copy in pair_copies(source, span, group * span, held, sems, group):
            copy.start()
    lane_head = lax.broadcasted_iota(jnp.int32, (GMAX, cols), 1) // HEAD_DIM
    block = min(512, span)
    is_key = lax.broadcasted_iota(jnp.int32, (heads * GMAX, block), 1) % 2 == 0
    placed = jnp.zeros(out_ref.shape, jnp.float32)
    for group in range(groups):
        picker = picker_ref[pl.ds(group * GMAX, GMAX), :]
        query = jnp.dot(picker, query_ref[...], preferred_element_type=jnp.float32)
        spread = jnp.concatenate(
            [jnp.where(lane_head == head, query, 0.0) for head in range(heads)], axis=0
        ).astype(jnp.bfloat16)
        for copy in pair_copies(source, span, group * span, held, sems, group):
            copy.wait()

        def states_of(at):
            return jnp.concatenate(
                [held[group, half, pl.ds(at, block), :] for half in range(held.shape[1])], axis=1
            )

        top = jnp.full((heads * GMAX, 1), NEG, jnp.float32)
        for at in range(0, span, block):
            scores = lax.dot_general(
                spread, states_of(at), (((1,), (1,)), ((), ())), preferred_element_type=jnp.float32
            )
            scores = jnp.where(is_key, scores, NEG)
            scores_ref[:, pl.ds(at, block)] = scores
            top = jnp.maximum(top, jnp.max(scores, axis=1, keepdims=True))
        total = jnp.zeros((heads * GMAX, 1), jnp.float32)
        summed = jnp.zeros((heads * GMAX, cols), jnp.float32)
        for at in range(0, span, block):
            weights = jnp.where(is_key, jnp.exp(scores_ref[:, pl.ds(at, block)] - top), 0.0)
            total += jnp.sum(weights, axis=1, keepdims=True)
            moved = pltpu.roll(weights, 1, 1).astype(jnp.bfloat16)
            summed += jnp.dot(moved, states_of(at), preferred_element_type=jnp.float32)
        summed = summed / total
        context = jnp.zeros((GMAX, cols), jnp.float32)
        for head in range(heads):
            context += jnp.where(lane_head == head, summed[head * GMAX : (head + 1) * GMAX], 0.0)
        placed += lax.dot_general(
            picker,
            context.astype(jnp.bfloat16),
            (((0,), (0,)), ((), ())),
            preferred_element_type=jnp.float32,
        )
    out_ref[...] = placed.astype(jnp.bfloat16)


def group_parts(picker, queries, enc_kv):
    groups, positions, _, cols = enc_kv.shape
    heads = cols // HEAD_DIM
    return pl.pallas_call(
        group_kernel,
        out_shape=jax.ShapeDtypeStruct(queries.shape, jnp.bfloat16),
        in_specs=[
            pl.BlockSpec(memory_space=pltpu.VMEM),
            pl.BlockSpec(memory_space=pltpu.VMEM),
            pl.BlockSpec(memory_space=pl.ANY),
        ],
        out_specs=pl.BlockSpec(memory_space=pltpu.VMEM),
        scratch_shapes=[
            pltpu.VMEM((groups, cols // LANES, 2 * positions, LANES), jnp.bfloat16),
            pltpu.VMEM((heads * GMAX, 2 * positions), jnp.float32),
            pltpu.SemaphoreType.DMA((groups, cols // LANES)),
        ],
        compiler_params=pltpu.CompilerParams(vmem_limit_bytes=VMEM_LIMIT),
        name="group_parts",
    )(picker, queries, enc_kv)


def group_picker(group_of, groups_here):
    local_groups = lax.axis_index("req") * groups_here + jnp.arange(groups_here, dtype=jnp.int32)
    member = group_of[None, :] == local_groups[:, None]
    member_rank = jnp.cumsum(member.astype(jnp.int32), axis=1) - 1
    picker = member[:, None, :] & (
        member_rank[:, None, :] == jnp.arange(GMAX, dtype=jnp.int32)[None, :, None]
    )
    return picker.astype(jnp.bfloat16).reshape(groups_here * GMAX, -1)


def group_attention(cross_query, group_of, enc_kv, scale):
    scaled = (cross_query * scale).astype(jnp.bfloat16)
    every_query = lax.all_gather(scaled, "req", axis=0, tiled=True)
    picker = group_picker(group_of, enc_kv.shape[0])
    placed = group_parts(picker, every_query, enc_kv)
    return lax.psum_scatter(placed, "req", scatter_dimension=0, tiled=True)


def on_device(
    tokens,
    cache_len,
    page_table,
    page_live,
    group_of,
    kv_pool,
    enc_kv,
    w_self_in,
    w_self_out,
    w_cross_q,
    w_cross_out,
    self_gain,
    self_bias,
    cross_gain,
    cross_bias,
):
    rows_here = tokens.shape[0]
    width = tokens.shape[1]
    head_cols = kv_pool.shape[3]
    scale = HEAD_DIM ** (-0.5)
    full_in, full_out, full_query, full_cross = (
        lax.all_gather(w_self_in, "req", axis=0, tiled=True),
        lax.all_gather(w_self_out, "req", axis=1, tiled=True),
        lax.all_gather(w_cross_q, "req", axis=0, tiled=True),
        lax.all_gather(w_cross_out, "req", axis=1, tiled=True),
    )
    projected = jnp.dot(
        tokens, full_in.reshape(width, 3 * head_cols), preferred_element_type=jnp.float32
    )
    qkv = projected.astype(jnp.bfloat16).reshape(rows_here, 3, head_cols)
    self_ctx = paged_attention(
        qkv[:, 0], qkv[:, 1], qkv[:, 2], cache_len, page_table, page_live, kv_pool, scale
    )
    self_proj = head_total(jnp.dot(self_ctx, full_out, preferred_element_type=jnp.float32))
    h_first = layer_norm(tokens.astype(jnp.float32) + self_proj, self_gain, self_bias).astype(
        jnp.bfloat16
    )
    cross_query = jnp.dot(h_first, full_query, preferred_element_type=jnp.float32)
    cross_query = cross_query.astype(jnp.bfloat16)
    cross_ctx = group_attention(cross_query, group_of, enc_kv, scale)
    cross_proj = head_total(jnp.dot(cross_ctx, full_cross, preferred_element_type=jnp.float32))
    hidden_out = layer_norm(
        h_first.astype(jnp.float32) + cross_proj, cross_gain, cross_bias
    ).astype(jnp.bfloat16)
    return (hidden_out, qkv[:, 1:3])


def solution(mesh):
    return jax.shard_map(
        on_device,
        mesh=mesh,
        in_specs=(
            P("req", None),
            P("req"),
            P("req", None),
            P("req", None),
            P(),
            P("req", None, None, "head"),
            P("req", None, None, "head"),
            P("req", None, "head"),
            P("head", "req"),
            P("req", "head"),
            P("head", "req"),
            P(),
            P(),
            P(),
            P(),
        ),
        out_specs=(P("req", None), P("req", None, "head")),
        check_vma=False,
    )
```

```python
import functools

import jax
import jax.numpy as jnp
from jax import lax
from jax.experimental import pallas as pl
from jax.experimental.pallas import tpu as pltpu
from jax.sharding import PartitionSpec as P

HEAD_DIM = 64
GMAX = 16


def layer_norm(summed, gain_row, bias_row):
    center = summed - jnp.mean(summed, axis=-1, keepdims=True)
    spread = jnp.mean(center * center, axis=-1, keepdims=True)
    return center * lax.rsqrt(spread + 1e-05) * gain_row + bias_row


LANES = 128
NEG = -1e30
VMEM_LIMIT = 60 * 1024 * 1024
MESH = pl.DeviceIdType.MESH
IN_VMEM = pl.BlockSpec(memory_space=pltpu.VMEM)


def greet(peers):
    barrier = pltpu.get_barrier_semaphore()
    for peer in peers:
        pl.semaphore_signal(barrier, inc=1, device_id=peer, device_id_type=MESH)
    pl.semaphore_wait(barrier, len(peers))


def others(axis, size):
    me = lax.axis_index(axis)
    return [{axis: lax.rem(me + step, size)} for step in range(1, size)]


def send(source, target, send_sem, recv_sem, peer):
    copy = pltpu.make_async_remote_copy(
        src_ref=source,
        dst_ref=target,
        send_sem=send_sem,
        recv_sem=recv_sem,
        device_id=peer,
        device_id_type=MESH,
    )
    copy.start()
    return copy


def weights_kernel(size, tokens_ref, *refs):
    count = 4
    shards, qkv_ref = refs[:count], refs[count]
    fulls = (refs[2 * count],) + tuple(refs[count + 1 : 2 * count])
    send_sems, recv_sems, own_sems = refs[2 * count + 1 :]
    side = size // 4 if size % 4 == 0 else 1
    deep = size // side
    me = lax.axis_index("req")
    far, near = me // side, lax.rem(me, side)
    far_peers = [lax.rem(far + step, deep) * side + near for step in range(1, deep)]
    near_peers = [far * side + lax.rem(near + step, side) for step in range(1, side)]
    greet([{"req": peer} for peer in far_peers + near_peers])

    def place(which, owner):
        rows = shards[which].shape[0]
        if len(fulls[which].shape) == 3:
            return fulls[which].at[owner]
        return fulls[which].at[pl.ds(pl.multiple_of(owner * rows, rows), rows), :]

    first = [[], [], [], []]
    second = [[], [], [], []]
    own = []
    for which in range(count):
        keep = pltpu.make_async_copy(shards[which], place(which, me), own_sems.at[which])
        keep.start()
        own.append(keep)
        for index, peer in enumerate(far_peers + near_peers):
            first[which].append(
                send(
                    shards[which],
                    place(which, me),
                    send_sems.at[which, index],
                    recv_sems.at[which, index],
                    {"req": peer},
                )
            )

    def forward(which):
        index = deep - 1 + side - 1
        for step in range(1, deep):
            first[which][step - 1].wait_recv()
            owner = lax.rem(far - step + deep, deep) * side + near
            for peer in near_peers:
                second[which].append(
                    send(
                        place(which, owner),
                        place(which, owner),
                        send_sems.at[which, index],
                        recv_sems.at[which, index],
                        {"req": peer},
                    )
                )
                index += 1

    for which in range(count):
        forward(which)
    for which in range(count):
        own[which].wait()
        for copy in first[which][deep - 1 :]:
            copy.wait_recv()
        for copy in second[which]:
            copy.wait_recv()
        if which == 0:
            qkv_ref[...] = jnp.dot(
                tokens_ref[...], fulls[0][...], preferred_element_type=jnp.float32
            ).astype(qkv_ref.dtype)
    for which in range(count):
        for copy in first[which] + second[which]:
            copy.wait_send()


def gather_weights(size, tokens, w_in, w_query, w_out, w_cross):
    rows = tokens.shape[0]
    side = size // 4 if size % 4 == 0 else 1
    deep = size // side
    copies = (deep - 1) + (side - 1) + (deep - 1) * (side - 1)
    kind = jnp.bfloat16
    return pl.pallas_call(
        functools.partial(weights_kernel, size),
        out_shape=(
            jax.ShapeDtypeStruct((rows, w_in.shape[1]), kind),
            jax.ShapeDtypeStruct((size * w_query.shape[0], w_query.shape[1]), kind),
            jax.ShapeDtypeStruct((size,) + w_out.shape, kind),
            jax.ShapeDtypeStruct((size,) + w_cross.shape, kind),
        ),
        in_specs=[IN_VMEM] * 5,
        out_specs=(IN_VMEM,) * 4,
        scratch_shapes=[
            pltpu.VMEM((size * w_in.shape[0], w_in.shape[1]), kind),
            pltpu.SemaphoreType.DMA((4, copies)),
            pltpu.SemaphoreType.DMA((4, copies)),
            pltpu.SemaphoreType.DMA((4,)),
        ],
        compiler_params=pltpu.CompilerParams(
            collective_id=0, has_side_effects=True, vmem_limit_bytes=VMEM_LIMIT
        ),
        name="gather_weights",
    )(tokens, w_in, w_query, w_out, w_cross)


def spread_and_sum(heads_size, partial, slots_ref, send_sems, recv_sems):
    me = lax.axis_index("head")
    slots_ref[me] = partial.astype(slots_ref.dtype)
    copies = [
        send(slots_ref.at[me], slots_ref.at[me], send_sems.at[index], recv_sems.at[index], peer)
        for index, peer in enumerate(others("head", heads_size))
    ]
    for copy in copies:
        copy.wait()
    summed = slots_ref[0].astype(jnp.float32)
    for index in range(1, heads_size):
        summed += slots_ref[index].astype(jnp.float32)
    return summed


def first_kernel(size, heads_size, scale, ctx_ref, tokens_ref, w_out_ref, w_query_ref, gain_ref, bias_ref,
                 h_ref, queries_ref, slots_ref, head_send, head_recv, req_send, req_recv):
    greet(others("head", heads_size) + others("req", size))
    partial = jnp.dot(ctx_ref[...], w_out_ref[...], preferred_element_type=jnp.float32)
    summed = spread_and_sum(heads_size, partial, slots_ref, head_send, head_recv)
    h_first = layer_norm(
        tokens_ref[...].astype(jnp.float32) + summed, gain_ref[...], bias_ref[...]
    ).astype(jnp.bfloat16)
    h_ref[...] = h_first
    query = jnp.dot(h_first, w_query_ref[...], preferred_element_type=jnp.float32)
    query = query.astype(jnp.bfloat16).astype(jnp.float32) * scale
    rows = ctx_ref.shape[0]
    me = lax.axis_index("req")
    here = pl.ds(pl.multiple_of(me * rows, rows), rows)
    queries_ref[here, :] = query.astype(jnp.bfloat16)
    copies = [
        send(queries_ref.at[here, :], queries_ref.at[here, :], req_send.at[index], req_recv.at[index], peer)
        for index, peer in enumerate(others("req", size))
    ]
    for copy in copies:
        copy.wait()


def last_kernel(size, heads_size, placed_ref, h_ref, w_cross_ref, gain_ref, bias_ref,
                out_ref, blocks_ref, slots_ref, head_send, head_recv, req_send, req_recv):
    greet(others("head", heads_size) + others("req", size))
    rows = h_ref.shape[0]
    me = lax.axis_index("req")
    copies = []
    for index, peer in enumerate(others("req", size)):
        there = pl.ds(pl.multiple_of(peer["req"] * rows, rows), rows)
        copies.append(
            send(placed_ref.at[there, :], blocks_ref.at[me], req_send.at[index], req_recv.at[index], peer)
        )
    blocks_ref[me] = placed_ref[pl.ds(pl.multiple_of(me * rows, rows), rows), :]
    for copy in copies:
        copy.wait()
    ctx = blocks_ref[0].astype(jnp.float32)
    for index in range(1, size):
        ctx += blocks_ref[index].astype(jnp.float32)
    partial = jnp.dot(ctx.astype(jnp.bfloat16), w_cross_ref[...], preferred_element_type=jnp.float32)
    summed = spread_and_sum(heads_size, partial, slots_ref, head_send, head_recv)
    out_ref[...] = layer_norm(
        h_ref[...].astype(jnp.float32) + summed, gain_ref[...], bias_ref[...]
    ).astype(jnp.bfloat16)


def exchange_sems(size, heads_size):
    return [
        pltpu.SemaphoreType.DMA((heads_size - 1,)),
        pltpu.SemaphoreType.DMA((heads_size - 1,)),
        pltpu.SemaphoreType.DMA((size - 1,)),
        pltpu.SemaphoreType.DMA((size - 1,)),
    ]


def first_half(size, heads_size, scale, ctx, tokens, w_out, w_query, gain, bias):
    rows, width = tokens.shape
    cols = ctx.shape[1]
    return pl.pallas_call(
        functools.partial(first_kernel, size, heads_size, scale),
        out_shape=(
            jax.ShapeDtypeStruct((rows, width), jnp.bfloat16),
            jax.ShapeDtypeStruct((size * rows, cols), jnp.bfloat16),
        ),
        in_specs=[IN_VMEM] * 6,
        out_specs=(IN_VMEM,) * 2,
        scratch_shapes=[pltpu.VMEM((heads_size, rows, width), jnp.bfloat16)]
        + exchange_sems(size, heads_size),
        compiler_params=pltpu.CompilerParams(
            collective_id=1, has_side_effects=True, vmem_limit_bytes=VMEM_LIMIT
        ),
        name="first_half",
    )(ctx, tokens, w_out, w_query, gain.reshape(1, -1), bias.reshape(1, -1))


def last_half(size, heads_size, placed, h_first, w_cross, gain, bias):
    rows, width = h_first.shape
    cols = placed.shape[1]
    return pl.pallas_call(
        functools.partial(last_kernel, size, heads_size),
        out_shape=jax.ShapeDtypeStruct((rows, width), jnp.bfloat16),
        in_specs=[IN_VMEM] * 5,
        out_specs=IN_VMEM,
        scratch_shapes=[
            pltpu.VMEM((size, rows, cols), jnp.bfloat16),
            pltpu.VMEM((heads_size, rows, width), jnp.bfloat16),
        ]
        + exchange_sems(size, heads_size),
        compiler_params=pltpu.CompilerParams(
            collective_id=2, has_side_effects=True, vmem_limit_bytes=VMEM_LIMIT
        ),
        name="last_half",
    )(placed, h_first, w_cross, gain.reshape(1, -1), bias.reshape(1, -1))


def pair_copies(source, rows, start, held, sems, slot):
    return [
        pltpu.make_async_copy(
            source.at[pl.ds(start, rows), pl.ds(half * LANES, LANES)],
            held.at[slot, half],
            sems.at[slot, half],
        )
        for half in range(held.shape[1])
    ]


def page_kernel(valid_ref, query_ref, kv_ref, acc_ref, top_ref, total_ref, held, sems, *, batch):
    pages, page_rows, _, cols = kv_ref.shape
    heads = cols // HEAD_DIM
    span = 2 * page_rows
    source = kv_ref.reshape(pages * span, cols)
    steps = pages // batch
    rows = batch * span
    slots = held.shape[0]
    for step in range(min(slots, steps)):
        for copy in pair_copies(source, rows, step * rows, held, sems, step):
            copy.start()
    head_row = lax.broadcasted_iota(jnp.int32, (8, cols), 0)
    head_mask = head_row == lax.broadcasted_iota(jnp.int32, (8, cols), 1) // HEAD_DIM
    column = lax.broadcasted_iota(jnp.int32, (8 * batch, span), 1)
    is_key = column % 2 == 0

    def states_of(slot, page):
        return jnp.concatenate(
            [held[slot, half, pl.ds(page * span, span), :] for half in range(held.shape[1])], axis=1
        )

    def body(step, carry):
        slot = lax.rem(step, slots)
        for copy in pair_copies(source, rows, step * rows, held, sems, slot):
            copy.wait()
        stack, limits = [], []
        for page in range(batch):
            query = query_ref[pl.ds(step * batch + page, 1), :]
            spread = jnp.where(head_mask, jnp.broadcast_to(query, (8, cols)), 0.0).astype(jnp.bfloat16)
            stack.append(
                lax.dot_general(
                    spread,
                    states_of(slot, page),
                    (((1,), (1,)), ((), ())),
                    preferred_element_type=jnp.float32,
                )
            )
            limits.append(jnp.full((8, span), 2 * valid_ref[step * batch + page], jnp.int32))
        counted = is_key & (column < jnp.concatenate(limits, axis=0))
        scores = jnp.where(counted, jnp.concatenate(stack, axis=0), NEG)
        top = jnp.max(scores, axis=1, keepdims=True)
        weights = jnp.where(counted, jnp.exp(scores - top), 0.0)
        total = jnp.sum(weights, axis=1, keepdims=True)
        moved = pltpu.roll(weights, 1, 1).astype(jnp.bfloat16)
        accs, tops, totals = [], [], []
        for page in range(batch):
            mine = slice(8 * page, 8 * page + 8)
            summed = jnp.dot(moved[mine], states_of(slot, page), preferred_element_type=jnp.float32)
            for parts, value in ((accs, summed), (tops, top[mine]), (totals, total[mine])):
                parts.append(jnp.sum(jnp.where(head_mask, value, 0.0), axis=0, keepdims=True))
        here = pl.ds(pl.multiple_of(step * batch, batch), batch)
        acc_ref[here, :] = jnp.concatenate(accs, axis=0)
        top_ref[here, :] = jnp.concatenate(tops, axis=0)
        total_ref[here, :] = jnp.concatenate(totals, axis=0)

        @pl.when(step + slots < steps)
        def _():
            for copy in pair_copies(source, rows, (step + slots) * rows, held, sems, slot):
                copy.start()

        return carry

    lax.fori_loop(0, steps, body, 0)


def page_parts(page_valid, page_query, kv_pool):
    pages, page_rows, _, cols = kv_pool.shape
    batch = 16
    slots = min(4, pages // batch)
    part = jax.ShapeDtypeStruct((pages, cols), jnp.float32)
    return pl.pallas_call(
        functools.partial(page_kernel, batch=batch),
        out_shape=(part, part, part),
        in_specs=[
            pl.BlockSpec(memory_space=pltpu.SMEM),
            pl.BlockSpec(memory_space=pltpu.VMEM),
            pl.BlockSpec(memory_space=pl.ANY),
        ],
        out_specs=(pl.BlockSpec(memory_space=pltpu.VMEM),) * 3,
        scratch_shapes=[
            pltpu.VMEM((slots, cols // LANES, batch * 2 * page_rows, LANES), jnp.bfloat16),
            pltpu.SemaphoreType.DMA((slots, cols // LANES)),
        ],
        compiler_params=pltpu.CompilerParams(vmem_limit_bytes=VMEM_LIMIT),
        cost_estimate=pl.CostEstimate(
            flops=pages * 8 * 2 * page_rows * cols * 4,
            bytes_accessed=pages * page_rows * 4 * cols,
            transcendentals=pages * 16 * page_rows,
        ),
        name="page_parts",
    )(page_valid, page_query, kv_pool)


def paged_attention(query, new_key, new_value, cache_len, page_table, page_live, kv_pool, scale):
    pages_here, page_rows, _, head_cols = kv_pool.shape
    heads_here = head_cols // HEAD_DIM
    rows_here = query.shape[0]
    slots = page_table.shape[1]
    counts = (cache_len + page_rows - 1) // page_rows
    slot_index = jnp.arange(slots, dtype=jnp.int32)
    in_use = slot_index[None, :] < counts[:, None]
    hits = (
        page_table[:, :, None] == jnp.arange(pages_here, dtype=jnp.int32)[None, None, :]
    ) & in_use[:, :, None]
    owners = jnp.any(hits, axis=1)
    slot_valid = jnp.where(
        page_live == 1,
        jnp.clip(cache_len[:, None] - slot_index[None, :] * page_rows, 0, page_rows),
        0,
    )
    page_valid = jnp.sum(jnp.where(hits, slot_valid[:, :, None], 0), axis=(0, 1))
    owner_weights = owners.astype(jnp.float32)
    scaled = (query * scale).astype(jnp.bfloat16)
    page_query = jnp.dot(owners.T.astype(jnp.bfloat16), scaled, preferred_element_type=jnp.float32)
    page_sum, page_top, page_total = page_parts(page_valid, page_query, kv_pool)
    products = query.astype(jnp.float32) * new_key.astype(jnp.float32)
    new_score = jnp.sum(products.reshape(rows_here, heads_here, HEAD_DIM), axis=-1) * scale
    new_score = jnp.repeat(new_score, HEAD_DIM, axis=1)
    counted = owners & (page_valid > 0)[None, :]
    owner_top = jnp.max(jnp.where(counted[:, :, None], page_top[None, :, :], NEG), axis=1)
    top = jnp.maximum(owner_top, new_score)
    page_shift = jnp.dot(owner_weights.T, top, precision=lax.Precision.HIGHEST)
    factor = jnp.where((page_valid > 0)[:, None], jnp.exp(page_top - page_shift), 0.0)
    new_weight = jnp.exp(new_score - top)
    both = jnp.dot(
        owner_weights,
        jnp.concatenate([page_sum * factor, page_total * factor], axis=1),
        precision=lax.Precision.HIGHEST,
    )
    rounded_new = lax.optimization_barrier(new_weight.astype(jnp.bfloat16)).astype(jnp.float32)
    summed = both[:, :head_cols] + rounded_new * new_value.astype(jnp.float32)
    return (summed / (both[:, head_cols:] + new_weight)).astype(jnp.bfloat16)


def group_kernel(picker_ref, query_ref, kv_ref, out_ref, held, scores_ref, sems):
    groups, positions, _, cols = kv_ref.shape
    heads = cols // HEAD_DIM
    span = 2 * positions
    source = kv_ref.reshape(groups * span, cols)
    for group in range(groups):
        for copy in pair_copies(source, span, group * span, held, sems, group):
            copy.start()
    lane_head = lax.broadcasted_iota(jnp.int32, (GMAX, cols), 1) // HEAD_DIM
    block = min(512, span)
    is_key = lax.broadcasted_iota(jnp.int32, (heads * GMAX, block), 1) % 2 == 0
    placed = jnp.zeros(out_ref.shape, jnp.float32)
    for group in range(groups):
        picker = picker_ref[pl.ds(group * GMAX, GMAX), :]
        query = jnp.dot(picker, query_ref[...], preferred_element_type=jnp.float32)
        spread = jnp.concatenate(
            [jnp.where(lane_head == head, query, 0.0) for head in range(heads)], axis=0
        ).astype(jnp.bfloat16)
        for copy in pair_copies(source, span, group * span, held, sems, group):
            copy.wait()

        def states_of(at):
            return jnp.concatenate(
                [held[group, half, pl.ds(at, block), :] for half in range(held.shape[1])], axis=1
            )

        top = jnp.full((heads * GMAX, 1), NEG, jnp.float32)
        for at in range(0, span, block):
            scores = lax.dot_general(
                spread, states_of(at), (((1,), (1,)), ((), ())), preferred_element_type=jnp.float32
            )
            scores = jnp.where(is_key, scores, NEG)
            scores_ref[:, pl.ds(at, block)] = scores
            top = jnp.maximum(top, jnp.max(scores, axis=1, keepdims=True))
        total = jnp.zeros((heads * GMAX, 1), jnp.float32)
        summed = jnp.zeros((heads * GMAX, cols), jnp.float32)
        for at in range(0, span, block):
            weights = jnp.where(is_key, jnp.exp(scores_ref[:, pl.ds(at, block)] - top), 0.0)
            total += jnp.sum(weights, axis=1, keepdims=True)
            moved = pltpu.roll(weights, 1, 1).astype(jnp.bfloat16)
            summed += jnp.dot(moved, states_of(at), preferred_element_type=jnp.float32)
        summed = summed / total
        context = jnp.zeros((GMAX, cols), jnp.float32)
        for head in range(heads):
            context += jnp.where(lane_head == head, summed[head * GMAX : (head + 1) * GMAX], 0.0)
        placed += lax.dot_general(
            picker,
            context.astype(jnp.bfloat16),
            (((0,), (0,)), ((), ())),
            preferred_element_type=jnp.float32,
        )
    out_ref[...] = placed.astype(jnp.bfloat16)


def group_parts(picker, queries, enc_kv):
    groups, positions, _, cols = enc_kv.shape
    heads = cols // HEAD_DIM
    return pl.pallas_call(
        group_kernel,
        out_shape=jax.ShapeDtypeStruct(queries.shape, jnp.bfloat16),
        in_specs=[
            pl.BlockSpec(memory_space=pltpu.VMEM),
            pl.BlockSpec(memory_space=pltpu.VMEM),
            pl.BlockSpec(memory_space=pl.ANY),
        ],
        out_specs=pl.BlockSpec(memory_space=pltpu.VMEM),
        scratch_shapes=[
            pltpu.VMEM((groups, cols // LANES, 2 * positions, LANES), jnp.bfloat16),
            pltpu.VMEM((heads * GMAX, 2 * positions), jnp.float32),
            pltpu.SemaphoreType.DMA((groups, cols // LANES)),
        ],
        compiler_params=pltpu.CompilerParams(vmem_limit_bytes=VMEM_LIMIT),
        name="group_parts",
    )(picker, queries, enc_kv)


def group_picker(group_of, groups_here):
    local_groups = lax.axis_index("req") * groups_here + jnp.arange(groups_here, dtype=jnp.int32)
    member = group_of[None, :] == local_groups[:, None]
    member_rank = jnp.cumsum(member.astype(jnp.int32), axis=1) - 1
    picker = member[:, None, :] & (
        member_rank[:, None, :] == jnp.arange(GMAX, dtype=jnp.int32)[None, :, None]
    )
    return picker.astype(jnp.bfloat16).reshape(groups_here * GMAX, -1)


def on_device(
    size,
    heads_size,
    tokens,
    cache_len,
    page_table,
    page_live,
    group_of,
    kv_pool,
    enc_kv,
    w_self_in,
    w_self_out,
    w_cross_q,
    w_cross_out,
    self_gain,
    self_bias,
    cross_gain,
    cross_bias,
):
    rows_here = tokens.shape[0]
    width = tokens.shape[1]
    head_cols = kv_pool.shape[3]
    scale = HEAD_DIM ** (-0.5)
    projected, full_query, out_blocks, cross_blocks = gather_weights(
        size, tokens, w_self_in.reshape(w_self_in.shape[0], 3 * head_cols), w_cross_q, w_self_out, w_cross_out
    )
    full_out = out_blocks.transpose(1, 0, 2).reshape(head_cols, width)
    full_cross = cross_blocks.transpose(1, 0, 2).reshape(head_cols, width)
    qkv = projected.reshape(rows_here, 3, head_cols)
    self_ctx = paged_attention(
        projected[:, :head_cols],
        projected[:, head_cols : 2 * head_cols],
        projected[:, 2 * head_cols :],
        cache_len,
        page_table,
        page_live,
        kv_pool,
        scale,
    )
    h_first, every_query = first_half(
        size, heads_size, scale, self_ctx, tokens, full_out, full_query, self_gain, self_bias
    )
    placed = group_parts(group_picker(group_of, enc_kv.shape[0]), every_query, enc_kv)
    hidden_out = last_half(size, heads_size, placed, h_first, full_cross, cross_gain, cross_bias)
    return (hidden_out, qkv[:, 1:3])


def solution(mesh):
    return jax.shard_map(
        functools.partial(on_device, mesh.shape["req"], mesh.shape["head"]),
        mesh=mesh,
        in_specs=(
            P("req", None),
            P("req"),
            P("req", None),
            P("req", None),
            P(),
            P("req", None, None, "head"),
            P("req", None, None, "head"),
            P("req", None, "head"),
            P("head", "req"),
            P("req", "head"),
            P("head", "req"),
            P(),
            P(),
            P(),
            P(),
        ),
        out_specs=(P("req", None), P("req", None, "head")),
        check_vma=False,
    )
```

```python
import functools

import jax
import jax.numpy as jnp
from jax import lax
from jax.experimental import pallas as pl
from jax.experimental.pallas import tpu as pltpu
from jax.sharding import PartitionSpec as P

HEAD_DIM = 64
GMAX = 16


def layer_norm(summed, gain_row, bias_row):
    center = summed - jnp.mean(summed, axis=-1, keepdims=True)
    spread = jnp.mean(center * center, axis=-1, keepdims=True)
    return center * lax.rsqrt(spread + 1e-05) * gain_row + bias_row


LANES = 128
NEG = -1e30
VMEM_LIMIT = 60 * 1024 * 1024
MESH = pl.DeviceIdType.MESH
IN_VMEM = pl.BlockSpec(memory_space=pltpu.VMEM)


def greet(peers):
    barrier = pltpu.get_barrier_semaphore()
    for peer in peers:
        pl.semaphore_signal(barrier, inc=1, device_id=peer, device_id_type=MESH)
    pl.semaphore_wait(barrier, len(peers))


def others(axis, size):
    me = lax.axis_index(axis)
    return [{axis: lax.rem(me + step, size)} for step in range(1, size)]


def send(source, target, send_sem, recv_sem, peer):
    copy = pltpu.make_async_remote_copy(
        src_ref=source,
        dst_ref=target,
        send_sem=send_sem,
        recv_sem=recv_sem,
        device_id=peer,
        device_id_type=MESH,
    )
    copy.start()
    return copy


class Relay:
    def __init__(self, size, shards, fulls, send_sems, recv_sems, own_sems):
        self.side = size // 4 if size % 4 == 0 else 1
        self.deep = size // self.side
        self.shards, self.fulls = shards, fulls
        self.sems = (send_sems, recv_sems, own_sems)
        side, deep, me = self.side, self.deep, lax.axis_index("req")
        self.me, self.far, self.near = me, me // side, lax.rem(me, side)
        self.far_peers = [lax.rem(self.far + step, deep) * side + self.near for step in range(1, deep)]
        self.near_peers = [self.far * side + lax.rem(self.near + step, side) for step in range(1, side)]
        self.peers = self.far_peers + self.near_peers

    def place(self, which, owner):
        full, rows = self.fulls[which], self.shards[which].shape[0]
        if len(full.shape) == 3:
            return full.at[owner]
        return full.at[pl.ds(pl.multiple_of(owner * rows, rows), rows), :]

    def push(self, which, index, source, owner, peer):
        send_sems, recv_sems, _ = self.sems
        return send(
            source,
            self.place(which, owner),
            send_sems.at[which, index],
            recv_sems.at[which, index],
            {"req": peer},
        )

    def start(self):
        greet([{"req": peer} for peer in self.peers])
        self.first, self.second, self.own = [], [], []
        for which, shard in enumerate(self.shards):
            keep = pltpu.make_async_copy(shard, self.place(which, self.me), self.sems[2].at[which])
            keep.start()
            self.own.append(keep)
            self.first.append(
                [self.push(which, index, shard, self.me, peer) for index, peer in enumerate(self.peers)]
            )

    def forward(self):
        for which in range(len(self.shards)):
            index = len(self.peers)
            passed = []
            for step in range(1, self.deep):
                self.first[which][step - 1].wait_recv()
                owner = lax.rem(self.far - step + self.deep, self.deep) * self.side + self.near
                for peer in self.near_peers:
                    passed.append(self.push(which, index, self.place(which, owner), owner, peer))
                    index += 1
            self.second.append(passed)

    def finish(self):
        for which in range(len(self.shards)):
            self.own[which].wait()
            for copy in self.first[which][self.deep - 1 :] + self.second[which]:
                copy.wait_recv()
        for which in range(len(self.shards)):
            for copy in self.first[which] + self.second[which]:
                copy.wait_send()


def relay_sems(size, count):
    side = size // 4 if size % 4 == 0 else 1
    deep = size // side
    copies = (deep - 1) + (side - 1) + (deep - 1) * (side - 1)
    return [
        pltpu.SemaphoreType.DMA((count, copies)),
        pltpu.SemaphoreType.DMA((count, copies)),
        pltpu.SemaphoreType.DMA((count,)),
    ]


def project_kernel(size, tokens_ref, w_in_ref, qkv_ref, full_ref, *sems):
    relay = Relay(size, [w_in_ref], [full_ref], *sems)
    relay.start()
    relay.forward()
    relay.finish()
    qkv_ref[...] = jnp.dot(
        tokens_ref[...], full_ref[...], preferred_element_type=jnp.float32
    ).astype(qkv_ref.dtype)


def project(size, tokens, w_in):
    return pl.pallas_call(
        functools.partial(project_kernel, size),
        out_shape=jax.ShapeDtypeStruct((tokens.shape[0], w_in.shape[1]), jnp.bfloat16),
        in_specs=[IN_VMEM] * 2,
        out_specs=IN_VMEM,
        scratch_shapes=[pltpu.VMEM((size * w_in.shape[0], w_in.shape[1]), jnp.bfloat16)]
        + relay_sems(size, 1),
        compiler_params=pltpu.CompilerParams(
            collective_id=0, has_side_effects=True, vmem_limit_bytes=VMEM_LIMIT
        ),
        name="project",
    )(tokens, w_in)


def spread_and_sum(heads_size, partial, slots_ref, send_sems, recv_sems):
    me = lax.axis_index("head")
    slots_ref[me] = partial.astype(slots_ref.dtype)
    copies = [
        send(slots_ref.at[me], slots_ref.at[me], send_sems.at[index], recv_sems.at[index], peer)
        for index, peer in enumerate(others("head", heads_size))
    ]
    for copy in copies:
        copy.wait()
    summed = slots_ref[0].astype(jnp.float32)
    for index in range(1, heads_size):
        summed += slots_ref[index].astype(jnp.float32)
    return summed


def first_kernel(size, heads_size, scale, ctx_ref, tokens_ref, w_out_ref, w_query_ref, gain_ref, bias_ref,
                 h_ref, queries_ref, slots_ref, head_send, head_recv, req_send, req_recv):
    greet(others("head", heads_size) + others("req", size))
    partial = jnp.dot(ctx_ref[...], w_out_ref[...], preferred_element_type=jnp.float32)
    summed = spread_and_sum(heads_size, partial, slots_ref, head_send, head_recv)
    h_first = layer_norm(
        tokens_ref[...].astype(jnp.float32) + summed, gain_ref[...], bias_ref[...]
    ).astype(jnp.bfloat16)
    h_ref[...] = h_first
    query = jnp.dot(h_first, w_query_ref[...], preferred_element_type=jnp.float32)
    query = query.astype(jnp.bfloat16).astype(jnp.float32) * scale
    rows = ctx_ref.shape[0]
    me = lax.axis_index("req")
    here = pl.ds(pl.multiple_of(me * rows, rows), rows)
    queries_ref[here, :] = query.astype(jnp.bfloat16)
    copies = [
        send(queries_ref.at[here, :], queries_ref.at[here, :], req_send.at[index], req_recv.at[index], peer)
        for index, peer in enumerate(others("req", size))
    ]
    for copy in copies:
        copy.wait()


def last_kernel(size, heads_size, placed_ref, h_ref, w_cross_ref, gain_ref, bias_ref,
                out_ref, blocks_ref, slots_ref, head_send, head_recv, req_send, req_recv):
    greet(others("head", heads_size) + others("req", size))
    rows = h_ref.shape[0]
    me = lax.axis_index("req")
    copies = []
    for index, peer in enumerate(others("req", size)):
        there = pl.ds(pl.multiple_of(peer["req"] * rows, rows), rows)
        copies.append(
            send(placed_ref.at[there, :], blocks_ref.at[me], req_send.at[index], req_recv.at[index], peer)
        )
    blocks_ref[me] = placed_ref[pl.ds(pl.multiple_of(me * rows, rows), rows), :]
    for copy in copies:
        copy.wait()
    ctx = blocks_ref[0].astype(jnp.float32)
    for index in range(1, size):
        ctx += blocks_ref[index].astype(jnp.float32)
    partial = jnp.dot(ctx.astype(jnp.bfloat16), w_cross_ref[...], preferred_element_type=jnp.float32)
    summed = spread_and_sum(heads_size, partial, slots_ref, head_send, head_recv)
    out_ref[...] = layer_norm(
        h_ref[...].astype(jnp.float32) + summed, gain_ref[...], bias_ref[...]
    ).astype(jnp.bfloat16)


def exchange_sems(size, heads_size):
    return [
        pltpu.SemaphoreType.DMA((heads_size - 1,)),
        pltpu.SemaphoreType.DMA((heads_size - 1,)),
        pltpu.SemaphoreType.DMA((size - 1,)),
        pltpu.SemaphoreType.DMA((size - 1,)),
    ]


def first_half(size, heads_size, scale, ctx, tokens, w_out, w_query, gain, bias):
    rows, width = tokens.shape
    cols = ctx.shape[1]
    return pl.pallas_call(
        functools.partial(first_kernel, size, heads_size, scale),
        out_shape=(
            jax.ShapeDtypeStruct((rows, width), jnp.bfloat16),
            jax.ShapeDtypeStruct((size * rows, cols), jnp.bfloat16),
        ),
        in_specs=[IN_VMEM] * 6,
        out_specs=(IN_VMEM,) * 2,
        scratch_shapes=[pltpu.VMEM((heads_size, rows, width), jnp.bfloat16)]
        + exchange_sems(size, heads_size),
        compiler_params=pltpu.CompilerParams(
            collective_id=1, has_side_effects=True, vmem_limit_bytes=VMEM_LIMIT
        ),
        name="first_half",
    )(ctx, tokens, w_out, w_query, gain.reshape(1, -1), bias.reshape(1, -1))


def last_half(size, heads_size, placed, h_first, w_cross, gain, bias):
    rows, width = h_first.shape
    cols = placed.shape[1]
    return pl.pallas_call(
        functools.partial(last_kernel, size, heads_size),
        out_shape=jax.ShapeDtypeStruct((rows, width), jnp.bfloat16),
        in_specs=[IN_VMEM] * 5,
        out_specs=IN_VMEM,
        scratch_shapes=[
            pltpu.VMEM((size, rows, cols), jnp.bfloat16),
            pltpu.VMEM((heads_size, rows, width), jnp.bfloat16),
        ]
        + exchange_sems(size, heads_size),
        compiler_params=pltpu.CompilerParams(
            collective_id=2, has_side_effects=True, vmem_limit_bytes=VMEM_LIMIT
        ),
        name="last_half",
    )(placed, h_first, w_cross, gain.reshape(1, -1), bias.reshape(1, -1))


def pair_copies(source, rows, start, held, sems, slot):
    return [
        pltpu.make_async_copy(
            source.at[pl.ds(start, rows), pl.ds(half * LANES, LANES)],
            held.at[slot, half],
            sems.at[slot, half],
        )
        for half in range(held.shape[1])
    ]


def page_kernel(valid_ref, query_ref, kv_ref, w_out_ref, w_query_ref, acc_ref, top_ref, total_ref,
                out_blocks_ref, full_query_ref, held, sems, *relay_refs, batch, size):
    pages, page_rows, _, cols = kv_ref.shape
    heads = cols // HEAD_DIM
    span = 2 * page_rows
    source = kv_ref.reshape(pages * span, cols)
    steps = pages // batch
    rows = batch * span
    slots = held.shape[0]
    for step in range(min(slots, steps)):
        for copy in pair_copies(source, rows, step * rows, held, sems, step):
            copy.start()
    relay = Relay(size, [w_out_ref, w_query_ref], [out_blocks_ref, full_query_ref], *relay_refs)
    relay.start()
    head_row = lax.broadcasted_iota(jnp.int32, (8, cols), 0)
    head_mask = head_row == lax.broadcasted_iota(jnp.int32, (8, cols), 1) // HEAD_DIM
    column = lax.broadcasted_iota(jnp.int32, (8 * batch, span), 1)
    is_key = column % 2 == 0

    def states_of(slot, page):
        return jnp.concatenate(
            [held[slot, half, pl.ds(page * span, span), :] for half in range(held.shape[1])], axis=1
        )

    def body(step, carry):
        slot = lax.rem(step, slots)
        for copy in pair_copies(source, rows, step * rows, held, sems, slot):
            copy.wait()
        stack, limits = [], []
        for page in range(batch):
            query = query_ref[pl.ds(step * batch + page, 1), :]
            spread = jnp.where(head_mask, jnp.broadcast_to(query, (8, cols)), 0.0).astype(jnp.bfloat16)
            stack.append(
                lax.dot_general(
                    spread,
                    states_of(slot, page),
                    (((1,), (1,)), ((), ())),
                    preferred_element_type=jnp.float32,
                )
            )
            limits.append(jnp.full((8, span), 2 * valid_ref[step * batch + page], jnp.int32))
        counted = is_key & (column < jnp.concatenate(limits, axis=0))
        scores = jnp.where(counted, jnp.concatenate(stack, axis=0), NEG)
        top = jnp.max(scores, axis=1, keepdims=True)
        weights = jnp.where(counted, jnp.exp(scores - top), 0.0)
        total = jnp.sum(weights, axis=1, keepdims=True)
        moved = pltpu.roll(weights, 1, 1).astype(jnp.bfloat16)
        accs, tops, totals = [], [], []
        for page in range(batch):
            mine = slice(8 * page, 8 * page + 8)
            summed = jnp.dot(moved[mine], states_of(slot, page), preferred_element_type=jnp.float32)
            for parts, value in ((accs, summed), (tops, top[mine]), (totals, total[mine])):
                parts.append(jnp.sum(jnp.where(head_mask, value, 0.0), axis=0, keepdims=True))
        here = pl.ds(pl.multiple_of(step * batch, batch), batch)
        acc_ref[here, :] = jnp.concatenate(accs, axis=0)
        top_ref[here, :] = jnp.concatenate(tops, axis=0)
        total_ref[here, :] = jnp.concatenate(totals, axis=0)

        @pl.when(step + slots < steps)
        def _():
            for copy in pair_copies(source, rows, (step + slots) * rows, held, sems, slot):
                copy.start()

        return carry

    lax.fori_loop(0, steps // 2, body, 0)
    relay.forward()
    lax.fori_loop(steps // 2, steps, body, 0)
    relay.finish()


def page_parts(size, page_valid, page_query, kv_pool, w_out, w_query):
    pages, page_rows, _, cols = kv_pool.shape
    batch = 16
    slots = min(4, pages // batch)
    part = jax.ShapeDtypeStruct((pages, cols), jnp.float32)
    return pl.pallas_call(
        functools.partial(page_kernel, batch=batch, size=size),
        out_shape=(
            part,
            part,
            part,
            jax.ShapeDtypeStruct((size,) + w_out.shape, jnp.bfloat16),
            jax.ShapeDtypeStruct((size * w_query.shape[0], w_query.shape[1]), jnp.bfloat16),
        ),
        in_specs=[
            pl.BlockSpec(memory_space=pltpu.SMEM),
            pl.BlockSpec(memory_space=pltpu.VMEM),
            pl.BlockSpec(memory_space=pl.ANY),
            IN_VMEM,
            IN_VMEM,
        ],
        out_specs=(IN_VMEM,) * 5,
        scratch_shapes=[
            pltpu.VMEM((slots, cols // LANES, batch * 2 * page_rows, LANES), jnp.bfloat16),
            pltpu.SemaphoreType.DMA((slots, cols // LANES)),
        ]
        + relay_sems(size, 2),
        compiler_params=pltpu.CompilerParams(
            collective_id=3, has_side_effects=True, vmem_limit_bytes=VMEM_LIMIT
        ),
        cost_estimate=pl.CostEstimate(
            flops=pages * 8 * 2 * page_rows * cols * 4,
            bytes_accessed=pages * page_rows * 4 * cols,
            transcendentals=pages * 16 * page_rows,
        ),
        name="page_parts",
    )(page_valid, page_query, kv_pool, w_out, w_query)


def paged_attention(
    size, query, new_key, new_value, cache_len, page_table, page_live, kv_pool, w_out, w_query, scale
):
    pages_here, page_rows, _, head_cols = kv_pool.shape
    heads_here = head_cols // HEAD_DIM
    rows_here = query.shape[0]
    slots = page_table.shape[1]
    counts = (cache_len + page_rows - 1) // page_rows
    slot_index = jnp.arange(slots, dtype=jnp.int32)
    in_use = slot_index[None, :] < counts[:, None]
    hits = (
        page_table[:, :, None] == jnp.arange(pages_here, dtype=jnp.int32)[None, None, :]
    ) & in_use[:, :, None]
    owners = jnp.any(hits, axis=1)
    slot_valid = jnp.where(
        page_live == 1,
        jnp.clip(cache_len[:, None] - slot_index[None, :] * page_rows, 0, page_rows),
        0,
    )
    page_valid = jnp.sum(jnp.where(hits, slot_valid[:, :, None], 0), axis=(0, 1))
    owner_weights = owners.astype(jnp.float32)
    scaled = (query * scale).astype(jnp.bfloat16)
    page_query = jnp.dot(owners.T.astype(jnp.bfloat16), scaled, preferred_element_type=jnp.float32)
    page_sum, page_top, page_total, out_blocks, full_query = page_parts(
        size, page_valid, page_query, kv_pool, w_out, w_query
    )
    products = query.astype(jnp.float32) * new_key.astype(jnp.float32)
    new_score = jnp.sum(products.reshape(rows_here, heads_here, HEAD_DIM), axis=-1) * scale
    new_score = jnp.repeat(new_score, HEAD_DIM, axis=1)
    counted = owners & (page_valid > 0)[None, :]
    owner_top = jnp.max(jnp.where(counted[:, :, None], page_top[None, :, :], NEG), axis=1)
    top = jnp.maximum(owner_top, new_score)
    page_shift = jnp.dot(owner_weights.T, top, precision=lax.Precision.HIGHEST)
    factor = jnp.where((page_valid > 0)[:, None], jnp.exp(page_top - page_shift), 0.0)
    new_weight = jnp.exp(new_score - top)
    both = jnp.dot(
        owner_weights,
        jnp.concatenate([page_sum * factor, page_total * factor], axis=1),
        precision=lax.Precision.HIGHEST,
    )
    rounded_new = lax.optimization_barrier(new_weight.astype(jnp.bfloat16)).astype(jnp.float32)
    summed = both[:, :head_cols] + rounded_new * new_value.astype(jnp.float32)
    context = (summed / (both[:, head_cols:] + new_weight)).astype(jnp.bfloat16)
    return context, out_blocks, full_query


def group_kernel(size, picker_ref, query_ref, kv_ref, w_cross_ref, out_ref, cross_blocks_ref,
                 held, scores_ref, sems, *relay_refs):
    groups, positions, _, cols = kv_ref.shape
    heads = cols // HEAD_DIM
    span = 2 * positions
    source = kv_ref.reshape(groups * span, cols)
    for group in range(groups):
        for copy in pair_copies(source, span, group * span, held, sems, group):
            copy.start()
    relay = Relay(size, [w_cross_ref], [cross_blocks_ref], *relay_refs)
    relay.start()
    lane_head = lax.broadcasted_iota(jnp.int32, (GMAX, cols), 1) // HEAD_DIM
    block = min(512, span)
    is_key = lax.broadcasted_iota(jnp.int32, (heads * GMAX, block), 1) % 2 == 0
    placed = jnp.zeros(out_ref.shape, jnp.float32)
    for group in range(groups):
        if group == groups // 2:
            relay.forward()
        picker = picker_ref[pl.ds(group * GMAX, GMAX), :]
        query = jnp.dot(picker, query_ref[...], preferred_element_type=jnp.float32)
        spread = jnp.concatenate(
            [jnp.where(lane_head == head, query, 0.0) for head in range(heads)], axis=0
        ).astype(jnp.bfloat16)
        for copy in pair_copies(source, span, group * span, held, sems, group):
            copy.wait()

        def states_of(at):
            return jnp.concatenate(
                [held[group, half, pl.ds(at, block), :] for half in range(held.shape[1])], axis=1
            )

        top = jnp.full((heads * GMAX, 1), NEG, jnp.float32)
        for at in range(0, span, block):
            scores = lax.dot_general(
                spread, states_of(at), (((1,), (1,)), ((), ())), preferred_element_type=jnp.float32
            )
            scores = jnp.where(is_key, scores, NEG)
            scores_ref[:, pl.ds(at, block)] = scores
            top = jnp.maximum(top, jnp.max(scores, axis=1, keepdims=True))
        total = jnp.zeros((heads * GMAX, 1), jnp.float32)
        summed = jnp.zeros((heads * GMAX, cols), jnp.float32)
        for at in range(0, span, block):
            weights = jnp.where(is_key, jnp.exp(scores_ref[:, pl.ds(at, block)] - top), 0.0)
            total += jnp.sum(weights, axis=1, keepdims=True)
            moved = pltpu.roll(weights, 1, 1).astype(jnp.bfloat16)
            summed += jnp.dot(moved, states_of(at), preferred_element_type=jnp.float32)
        summed = summed / total
        context = jnp.zeros((GMAX, cols), jnp.float32)
        for head in range(heads):
            context += jnp.where(lane_head == head, summed[head * GMAX : (head + 1) * GMAX], 0.0)
        placed += lax.dot_general(
            picker,
            context.astype(jnp.bfloat16),
            (((0,), (0,)), ((), ())),
            preferred_element_type=jnp.float32,
        )
    out_ref[...] = placed.astype(jnp.bfloat16)
    relay.finish()


def group_parts(size, picker, queries, enc_kv, w_cross):
    groups, positions, _, cols = enc_kv.shape
    heads = cols // HEAD_DIM
    return pl.pallas_call(
        functools.partial(group_kernel, size),
        out_shape=(
            jax.ShapeDtypeStruct(queries.shape, jnp.bfloat16),
            jax.ShapeDtypeStruct((size,) + w_cross.shape, jnp.bfloat16),
        ),
        in_specs=[
            pl.BlockSpec(memory_space=pltpu.VMEM),
            pl.BlockSpec(memory_space=pltpu.VMEM),
            pl.BlockSpec(memory_space=pl.ANY),
            IN_VMEM,
        ],
        out_specs=(IN_VMEM,) * 2,
        scratch_shapes=[
            pltpu.VMEM((groups, cols // LANES, 2 * positions, LANES), jnp.bfloat16),
            pltpu.VMEM((heads * GMAX, 2 * positions), jnp.float32),
            pltpu.SemaphoreType.DMA((groups, cols // LANES)),
        ]
        + relay_sems(size, 1),
        compiler_params=pltpu.CompilerParams(
            collective_id=4, has_side_effects=True, vmem_limit_bytes=VMEM_LIMIT
        ),
        name="group_parts",
    )(picker, queries, enc_kv, w_cross)


def group_picker(group_of, groups_here):
    local_groups = lax.axis_index("req") * groups_here + jnp.arange(groups_here, dtype=jnp.int32)
    member = group_of[None, :] == local_groups[:, None]
    member_rank = jnp.cumsum(member.astype(jnp.int32), axis=1) - 1
    picker = member[:, None, :] & (
        member_rank[:, None, :] == jnp.arange(GMAX, dtype=jnp.int32)[None, :, None]
    )
    return picker.astype(jnp.bfloat16).reshape(groups_here * GMAX, -1)


def on_device(
    size,
    heads_size,
    tokens,
    cache_len,
    page_table,
    page_live,
    group_of,
    kv_pool,
    enc_kv,
    w_self_in,
    w_self_out,
    w_cross_q,
    w_cross_out,
    self_gain,
    self_bias,
    cross_gain,
    cross_bias,
):
    rows_here = tokens.shape[0]
    width = tokens.shape[1]
    head_cols = kv_pool.shape[3]
    scale = HEAD_DIM ** (-0.5)
    projected = project(size, tokens, w_self_in.reshape(w_self_in.shape[0], 3 * head_cols))
    qkv = projected.reshape(rows_here, 3, head_cols)
    self_ctx, out_blocks, full_query = paged_attention(
        size,
        projected[:, :head_cols],
        projected[:, head_cols : 2 * head_cols],
        projected[:, 2 * head_cols :],
        cache_len,
        page_table,
        page_live,
        kv_pool,
        w_self_out,
        w_cross_q,
        scale,
    )
    full_out = out_blocks.transpose(1, 0, 2).reshape(head_cols, width)
    h_first, every_query = first_half(
        size, heads_size, scale, self_ctx, tokens, full_out, full_query, self_gain, self_bias
    )
    placed, cross_blocks = group_parts(
        size, group_picker(group_of, enc_kv.shape[0]), every_query, enc_kv, w_cross_out
    )
    full_cross = cross_blocks.transpose(1, 0, 2).reshape(head_cols, width)
    hidden_out = last_half(size, heads_size, placed, h_first, full_cross, cross_gain, cross_bias)
    return (hidden_out, qkv[:, 1:3])


def solution(mesh):
    return jax.shard_map(
        functools.partial(on_device, mesh.shape["req"], mesh.shape["head"]),
        mesh=mesh,
        in_specs=(
            P("req", None),
            P("req"),
            P("req", None),
            P("req", None),
            P(),
            P("req", None, None, "head"),
            P("req", None, None, "head"),
            P("req", None, "head"),
            P("head", "req"),
            P("req", "head"),
            P("head", "req"),
            P(),
            P(),
            P(),
            P(),
        ),
        out_specs=(P("req", None), P("req", None, "head")),
        check_vma=False,
    )
```
